32 devices in a mesh: groups: 2 (over x), seq: 16 (over z, y, core).
Axes of the slice: x: 2, y: 2, z: 4, core: 2. Of those that a mesh axis runs over, the one named last changes fastest.
Arguments:
- prompt_query: bfloat16 [4096, 4096], P(('groups', 'seq')), parts along dimension 0, may hold values from -16 to 16
- prompt_key: bfloat16 [4096, 4096], P(('groups', 'seq')), parts along dimension 0, may hold values from -16 to 16
- prompt_value: bfloat16 [4096, 4096], P(('groups', 'seq')), parts along dimension 0, may hold values from -6 to 6
- response_embed: bfloat16 [1024, 4096], P('groups'), parts along dimension 0, may hold values from -32 to 32
- mask_embed: bfloat16 [4096], replicated, may hold values from -6 to 6
- commit_step: int32 [1024], P('groups'), parts along dimension 0, may hold values from 1 to 4
- block_index: int32 [2], P('groups'), parts along dimension 0, may hold values from 0 to 7
- attention_gain: bfloat16 [4096], replicated, may hold values from 0.099609375 to 1.8984375
- residual_gain: bfloat16 [4096], replicated, may hold values from 0.099609375 to 1.8984375
- query_weight: bfloat16 [4096, 4096], P(None, 'seq'), may hold values from -0.125 to 0.125
- key_weight: bfloat16 [4096, 4096], P(None, 'seq'), may hold values from -0.09375 to 0.09375
- value_weight: bfloat16 [4096, 4096], P(None, 'seq'), may hold values from -1.5 to 1.5
- output_weight: bfloat16 [4096, 4096], P('seq'), may hold values from -0.09375 to 0.09375
Outputs:
- prompt_context: bfloat16 [4096, 4096], P(('groups', 'seq')), parts along dimension 0
- response_residual: bfloat16 [4, 1024, 4096], P(None, ('groups', 'seq')), parts along dimension 1
- response_normed: bfloat16 [4, 1024, 4096], P(None, ('groups', 'seq')), parts along dimension 1
The draws below stay inside these ranges and needn't reach their ends.
There are 2 independent parts, one for each index of `groups`. The reference program is written for one: setup_inputs(seed, part) draws one part's arguments, and reference() takes and returns one part's arrays. A program takes and returns all parts, laid end to end along the dimension named above; an argument that names none is the same for every part. Nothing has to cross between parts.
All inputs are finite; a program needn't handle non-finite values.
Results may differ from the reference program's by a relative error of at most 0.018.
Values may be sent and summed in bfloat16 or wider, within the bound.
A program may use at most 128 MiB of HBM per device.

```python
import math
import jax
import jax.numpy as jnp
from jax import lax

D = 4096
HEADS = 32
HD = 128
RESP = 512
STEPS = 4
BLOCKS = 8
PROMPT = 2048


def draw_prompt_query(key, part):
    values = jnp.clip(jax.random.normal(jax.random.fold_in(key, 11), (PROMPT, HEADS * HD), jnp.float32), -4.0, 4.0) * 1.6
    return values.astype(jnp.bfloat16)


def draw_prompt_key(key, part):
    values = jnp.clip(jax.random.normal(jax.random.fold_in(key, 13), (PROMPT, HEADS * HD), jnp.float32), -4.0, 4.0) * 1.6
    return values.astype(jnp.bfloat16)


def draw_response_embed(key, part):
    row_scale = jnp.exp(jax.random.uniform(jax.random.fold_in(key, 21), (RESP, 1), jnp.float32, minval=-1.15, maxval=1.15))
    col_scale = jnp.exp(jax.random.uniform(jax.random.fold_in(key, 22), (1, D), jnp.float32, minval=-0.8, maxval=0.8))
    core = jnp.clip(jax.random.normal(jax.random.fold_in(key, 23), (RESP, D), jnp.float32), -4.0, 4.0)
    return (core * row_scale * col_scale).astype(jnp.bfloat16)


def place_ends(values, own_key, low, top_value):
    dims = values.shape
    spot = [jax.random.randint(jax.random.fold_in(own_key, axis), (), 0, dims[axis]) for axis in range(len(dims))]
    values = values.at[tuple(spot)].set(low)
    longest = dims.index(max(dims))
    spot[longest] = (spot[longest] + 1) % dims[longest]
    return values.at[tuple(spot)].set(top_value)


def level_of(own_key, extent, pieces, smallest, top_value):
    factor_of = 1.0
    for position, shards_of in pieces:
        heights = jax.random.uniform(jax.random.fold_in(jax.random.fold_in(own_key, 6), position), (shards_of,), jnp.float32, smallest / len(pieces), top_value / len(pieces))
        factor_of = factor_of * jnp.repeat(jnp.exp(heights), extent[position] // shards_of).reshape((-1,) + (1,) * (len(extent) - 1 - position))
    return factor_of


def bell_draw(own_key, dims, scale, bound, pieces=(), kind=jnp.bfloat16):
    values = scale * jax.random.normal(own_key, dims, jnp.float32)
    if pieces:
        values = values * level_of(own_key, dims, pieces, -0.22, 0.18)
    return jnp.clip(values, -bound, bound).astype(kind)


def setup_inputs(seed: int = 0, part: int = 0) -> dict:
    arg_keys = jax.random.split(jax.random.key(seed), 14)
    part_keys = jax.random.split(jax.random.fold_in(arg_keys[13], part), 14)
    return {
        "prompt_query": draw_prompt_query(jax.random.fold_in(jax.random.fold_in(arg_keys[13], part), 71), part),
        "prompt_key": draw_prompt_key(jax.random.fold_in(jax.random.fold_in(arg_keys[13], part), 71), part),
        "prompt_value": bell_draw(part_keys[2], (PROMPT, HEADS * HD), 1.0, 6.0, ((0, 16),)),
        "response_embed": draw_response_embed(jax.random.fold_in(jax.random.fold_in(arg_keys[13], part), 71), part),
        "mask_embed": bell_draw(arg_keys[4], (D,), 1.0, 6.0),
        "commit_step": place_ends(jax.random.randint(part_keys[5], (RESP,), 1, STEPS + 1), jax.random.fold_in(part_keys[5], 1), 1, STEPS).astype(jnp.int32),
        "block_index": jax.random.randint(part_keys[6], (1,), 0, BLOCKS).astype(jnp.int32),
        "attention_gain": jnp.clip(1.0 + 0.18 * jax.random.normal(arg_keys[7], (D,), jnp.float32), 0.099609375, 1.8984375).astype(jnp.bfloat16),
        "residual_gain": jnp.clip(1.0 + 0.18 * jax.random.normal(arg_keys[8], (D,), jnp.float32), 0.099609375, 1.8984375).astype(jnp.bfloat16),
        "query_weight": bell_draw(arg_keys[9], (D, HEADS * HD), (D // 2) ** -0.5, 0.125, ((1, 16),)),
        "key_weight": bell_draw(arg_keys[10], (D, HEADS * HD), D ** -0.5, 0.09375, ((1, 16),)),
        "value_weight": bell_draw(arg_keys[11], (D, HEADS * HD), (max(1, D // 256)) ** -0.5, 1.5, ((1, 16),)),
        "output_weight": bell_draw(arg_keys[12], (HEADS * HD, D), (HEADS * HD) ** -0.5, 0.09375, ((0, 16),)),
    }


rope_base = 500000.0
norm_eps = 1e-05

def rotary(vectors, positions):
    half_size = vectors.shape[-1] // 2
    exponent = jnp.arange(half_size, dtype=jnp.float32) * (2.0 / vectors.shape[-1])
    inv_freq = rope_base ** (-exponent)
    angles = positions.astype(jnp.float32)[:, None] * inv_freq[None, :]
    cosine = jnp.cos(angles)[:, None, :]
    sine_part = jnp.sin(angles)[:, None, :]
    first_half = vectors[..., :half_size]
    second = vectors[..., half_size:]
    return jnp.concatenate([first_half * cosine - second * sine_part, second * cosine + first_half * sine_part], axis=-1)

def rms_scale(row_values, gain_row):
    return row_values * lax.rsqrt(lax.optimization_barrier(jnp.mean(row_values * row_values, axis=-1, keepdims=True)) + norm_eps) * gain_row.astype(jnp.float32)

def attend_one(queries, all_keys, all_values):
    score_scale = 1.0 / math.sqrt(queries.shape[-1])
    scores = jnp.dot(queries, all_keys.T, preferred_element_type=jnp.float32) * score_scale
    row_max = lax.optimization_barrier(jnp.max(scores, axis=-1, keepdims=True))
    weights = jnp.exp(scores - row_max)
    row_total = lax.optimization_barrier(jnp.sum(weights, axis=-1))
    weighted = jnp.dot(weights.astype(jnp.bfloat16), all_values, preferred_element_type=jnp.float32)
    return (weighted / row_total[:, None]).astype(jnp.bfloat16)

def attend_heads(queries, all_keys, all_values):
    head_q = jnp.transpose(queries, (1, 0, 2))
    head_k = jnp.transpose(all_keys, (1, 0, 2))
    head_v = jnp.transpose(all_values, (1, 0, 2))
    result = lax.map(lambda trio: attend_one(trio[0], trio[1], trio[2]), (head_q, head_k, head_v))
    return jnp.transpose(result, (1, 0, 2))

def reference(prompt_query, prompt_key, prompt_value, response_embed, mask_embed, commit_step, block_index, attention_gain, residual_gain, query_weight, key_weight, value_weight, output_weight):
    prompt_len = prompt_query.shape[0]
    resp_len = response_embed.shape[0]
    prompt_pos = jnp.arange(prompt_len, dtype=jnp.int32)
    resp_pos = (prompt_len + block_index[0] * resp_len + jnp.arange(resp_len, dtype=jnp.int32)).astype(jnp.int32)
    rot_query = rotary(prompt_query.astype(jnp.float32).reshape(prompt_len, HEADS, HD), prompt_pos).astype(jnp.bfloat16)
    rot_key = rotary(prompt_key.astype(jnp.float32).reshape(prompt_len, HEADS, HD), prompt_pos).astype(jnp.bfloat16)
    plain_value = prompt_value.reshape(prompt_len, HEADS, HD)
    residuals = []
    normed_rows = []
    prompt_out = None
    for step_index in range(STEPS):
        shown = (commit_step <= step_index)[:, None]
        step_input = jnp.where(shown, response_embed, mask_embed[None, :])
        input_f32 = step_input.astype(jnp.float32)
        normed_in = rms_scale(input_f32, attention_gain).astype(jnp.bfloat16)
        resp_query = rotary(jnp.dot(normed_in, query_weight, preferred_element_type=jnp.float32).reshape(resp_len, HEADS, HD), resp_pos).astype(jnp.bfloat16)
        resp_key = rotary(jnp.dot(normed_in, key_weight, preferred_element_type=jnp.float32).reshape(resp_len, HEADS, HD), resp_pos).astype(jnp.bfloat16)
        resp_value = jnp.dot(normed_in, value_weight, preferred_element_type=jnp.float32).astype(jnp.bfloat16).reshape(resp_len, HEADS, HD)
        all_keys = jnp.concatenate([rot_key, resp_key], axis=0)
        all_values = jnp.concatenate([plain_value, resp_value], axis=0)
        if step_index == 0:
            prompt_out = attend_heads(rot_query, all_keys, all_values).reshape(prompt_len, HEADS * HD)
        context = attend_heads(resp_query, all_keys, all_values).reshape(resp_len, HEADS * HD)
        attn_out = jnp.dot(context, output_weight, preferred_element_type=jnp.float32)
        hidden = input_f32 + attn_out
        residuals.append(hidden.astype(jnp.bfloat16))
        normed_rows.append(rms_scale(hidden, residual_gain).astype(jnp.bfloat16))
    return (prompt_out, jnp.stack(residuals), jnp.stack(normed_rows))
```

```python
import functools
import math

import jax
import jax.numpy as jnp
from jax import lax
from jax.experimental import pallas as pl
from jax.experimental.pallas import tpu as pltpu
from jax.sharding import PartitionSpec as P

HD = 128
STEPS = 4
ROPE_BASE = 500000.0
NORM_EPS = 1e-05
QBLOCK = 256
VMEM_LIMIT = 48 * 1024 * 1024
NT = (((1,), (1,)), ((), ()))


def rope_tables(positions):
    half = HD // 2
    exponent = jnp.arange(half, dtype=jnp.float32) * (2.0 / HD)
    inv_freq = ROPE_BASE ** (-exponent)
    angles = positions.astype(jnp.float32)[:, None] * inv_freq[None, :]
    cosine = jnp.cos(angles)
    sine = jnp.sin(angles)
    return jnp.concatenate([cosine, cosine], axis=-1), jnp.concatenate([-sine, sine], axis=-1)


def rms_scale(row_values, gain_row):
    return (
        row_values
        * lax.rsqrt(jnp.mean(row_values * row_values, axis=-1, keepdims=True) + NORM_EPS)
        * gain_row.astype(jnp.float32)
    )


def rope_in(x, cosine, sine):
    return x * cosine + pltpu.roll(x, HD // 2, 1) * sine


def query_factor():
    return math.log2(math.e) / math.sqrt(HD)


def kv_prep_kernel(key_ref, value_ref, cos_ref, sin_ref, kv_ref):
    for h in range(key_ref.shape[1] // HD):
        cols = slice(h * HD, (h + 1) * HD)
        kv_ref[0, 0, :, cols] = rope_in(
            key_ref[:, cols].astype(jnp.float32), cos_ref[...], sin_ref[...]
        ).astype(jnp.bfloat16)
    kv_ref[0, 1] = value_ref[...]


def q_prep_kernel(query_ref, cos_ref, sin_ref, q_ref):
    for h in range(query_ref.shape[1] // HD):
        cols = slice(h * HD, (h + 1) * HD)
        turned = rope_in(query_ref[:, cols].astype(jnp.float32), cos_ref[...], sin_ref[...])
        q_ref[0, :, cols] = (turned * query_factor()).astype(jnp.bfloat16)


def response_kernel(
    q_ref, k_ref, v_ref, kv_ref, cos_ref, sin_ref, commit_ref,
    out_ref, key0_ref, value0_ref,
    q_both, k_both, v_both, prompt_va, step_va, part_o, part_m,
):
    resp = cos_ref.shape[0]
    shards, _, rows, _ = kv_ref.shape
    prompt = shards * rows
    cosine, sine = cos_ref[...], sin_ref[...]

    def both(ref, dest, turn, factor):
        shown = ref[pl.ds(0, resp), :]
        hidden = jnp.broadcast_to(ref[pl.ds(resp, 1), :], (resp, HD))
        for slot, x in ((0, hidden), (1, shown)):
            if turn:
                x = rope_in(x, cosine, sine)
            dest[pl.ds(slot * resp, resp), :] = (x * factor).astype(jnp.bfloat16).astype(jnp.float32)

    both(q_ref, q_both, True, query_factor())
    both(k_ref, k_both, True, 1.0)
    both(v_ref, v_both, False, 1.0)
    prompt_va[:, :HD] = kv_ref[:, 1].reshape(prompt, HD)
    prompt_va[:, HD:] = jnp.ones((prompt, HD), jnp.bfloat16)
    step_va[:, HD:] = jnp.ones((resp, HD), jnp.bfloat16)
    block = math.gcd(QBLOCK, resp)

    def prompt_part(i, carry):
        at = pl.ds(pl.multiple_of(i * block, block), block)
        q = q_both[at, :].astype(jnp.bfloat16)
        k = kv_ref[:, 0].reshape(prompt, HD)
        s = lax.dot_general(q, k, NT, preferred_element_type=jnp.float32)
        m = jnp.max(s, axis=-1, keepdims=True)
        p = jnp.exp2(s - m).astype(jnp.bfloat16)
        part_o[at, :] = jnp.dot(p, prompt_va[...], preferred_element_type=jnp.float32)
        part_m[at, :] = jnp.broadcast_to(m, (block, HD))
        return carry

    lax.fori_loop(0, 2 * resp // block, prompt_part, 0)
    out_rows = out_ref.shape[2]
    for step in range(STEPS):
        shown = commit_ref[...] <= step
        k_s = jnp.where(shown, k_both[resp:, :], k_both[:resp, :]).astype(jnp.bfloat16)
        v_s = jnp.where(shown, v_both[resp:, :], v_both[:resp, :]).astype(jnp.bfloat16)
        step_va[:, :HD] = v_s
        if step == 0:
            key0_ref[...] = k_s
            value0_ref[...] = v_s
        for i in range(resp // block):
            lo, hi = i * block, (i + 1) * block
            here = commit_ref[lo:hi, :] <= step

            def pick(ref):
                return jnp.where(here, ref[resp + lo : resp + hi, :HD], ref[lo:hi, :HD])

            q = pick(q_both).astype(jnp.bfloat16)
            s = lax.dot_general(q, k_s, NT, preferred_element_type=jnp.float32)
            m_prompt = pick(part_m)
            m = jnp.maximum(jnp.max(s, axis=-1, keepdims=True), m_prompt)
            p = jnp.exp2(s - m[:, :1]).astype(jnp.bfloat16)
            o = jnp.dot(p, step_va[...], preferred_element_type=jnp.float32)
            shrink = jnp.exp2(m_prompt - m)
            top = o[:, :HD] + shrink * pick(part_o)
            total = o[:, HD:] + shrink * jnp.where(
                here, part_o[resp + lo : resp + hi, HD:], part_o[lo:hi, HD:]
            )
            out_ref[lo // out_rows : hi // out_rows, step] = (
                (top / total).astype(jnp.bfloat16).reshape(block // out_rows, out_rows, HD)
            )


def prompt_kernel(q_ref, kv_ref, key0_ref, value0_ref, out_ref, va):
    shards, _, rows, _ = kv_ref.shape
    prompt = shards * rows

    @pl.when(pl.program_id(1) == 0)
    def _():
        va[:prompt, :HD] = kv_ref[:, 1].reshape(prompt, HD)
        va[prompt:, :HD] = value0_ref[...]
        va[:, HD:] = jnp.ones((va.shape[0], HD), jnp.bfloat16)

    q = q_ref[...].reshape(-1, HD)
    s1 = lax.dot_general(
        q, kv_ref[:, 0].reshape(prompt, HD), NT, preferred_element_type=jnp.float32
    )
    s2 = lax.dot_general(q, key0_ref[...], NT, preferred_element_type=jnp.float32)
    m = jnp.maximum(jnp.max(s1, axis=-1, keepdims=True), jnp.max(s2, axis=-1, keepdims=True))
    p1 = jnp.exp2(s1 - m).astype(jnp.bfloat16)
    p2 = jnp.exp2(s2 - m).astype(jnp.bfloat16)
    o = jnp.dot(p1, va[:prompt, :], preferred_element_type=jnp.float32)
    o += jnp.dot(p2, va[prompt:, :], preferred_element_type=jnp.float32)
    out_ref[...] = (o[:, :HD] / o[:, HD:]).astype(jnp.bfloat16).reshape(out_ref.shape)


def per_device(
    prompt_query, prompt_key, prompt_value, response_embed, mask_embed, commit_step, block_index,
    attention_gain, residual_gain, query_weight, key_weight, value_weight, output_weight,
):
    rows, width = prompt_query.shape
    resp = response_embed.shape[0]
    model = response_embed.shape[1]
    shards = lax.axis_size("seq")
    groups = lax.axis_size("groups")
    me = lax.axis_index("seq")
    group = lax.axis_index("groups")
    cores = 2
    core = lax.rem(me, cores)
    local = query_weight.shape[1]
    heads = local // HD
    prompt = rows * shards
    params = pltpu.CompilerParams(vmem_limit_bytes=VMEM_LIMIT)
    swap = [(i, i ^ 1) for i in range(shards)]

    depth = output_weight.shape[0]
    share = model // (groups * cores)
    own_w = lax.dynamic_slice_in_dim(output_weight, (group * cores + core) * share, share, 1)
    give_w = lax.dynamic_slice_in_dim(output_weight, (group * cores + 1 - core) * share, share, 1)

    cos_p, sin_p = rope_tables(me * rows + jnp.arange(rows, dtype=jnp.int32))
    table = pl.BlockSpec((rows, HD), lambda s: (0, 0))
    column = pl.BlockSpec((rows, local), lambda s: (0, s))
    kv = pl.pallas_call(
        kv_prep_kernel,
        grid=(shards,),
        in_specs=[column, column, table, table],
        out_specs=pl.BlockSpec((1, 2, rows, local), lambda s: (s, 0, 0, 0)),
        out_shape=jax.ShapeDtypeStruct((shards, 2, rows, local), jnp.bfloat16),
        compiler_params=params,
    )(prompt_key, prompt_value, cos_p, sin_p)
    kv = lax.all_to_all(kv, "seq", split_axis=0, concat_axis=0)
    q_sent = pl.pallas_call(
        q_prep_kernel,
        grid=(shards,),
        in_specs=[column, table, table],
        out_specs=pl.BlockSpec((1, rows, local), lambda s: (s, 0, 0)),
        out_shape=jax.ShapeDtypeStruct((shards, rows, local), jnp.bfloat16),
        compiler_params=params,
    )(prompt_query, cos_p, sin_p)
    q = lax.all_to_all(q_sent, "seq", split_axis=0, concat_axis=0)

    got_w = lax.ppermute(give_w, "seq", swap)
    pair_w = jnp.where(core == 0, jnp.stack([own_w, got_w]), jnp.stack([got_w, own_w]))
    same_core = [[i for i in range(shards) if i % cores == c] for c in range(cores)]
    all_w = lax.all_gather(pair_w, "seq", axis=0, tiled=True, axis_index_groups=same_core)
    all_w = all_w.reshape(width, share)

    both = jnp.concatenate(
        [response_embed, jnp.broadcast_to(mask_embed[None, :], (16, model))], axis=0
    )
    normed = rms_scale(both.astype(jnp.float32), attention_gain).astype(jnp.bfloat16)
    proj = [
        jnp.dot(normed, w, preferred_element_type=jnp.float32)
        for w in (query_weight, key_weight, value_weight)
    ]
    cos_r, sin_r = rope_tables(prompt + block_index[0] * resp + jnp.arange(resp, dtype=jnp.int32))
    commit_wide = jnp.broadcast_to(commit_step[:, None], (resp, HD))

    out_rows = resp // shards
    head_col = pl.BlockSpec((resp + 16, HD), lambda h: (0, h))
    full = pl.BlockSpec((resp, HD), lambda h: (0, 0))
    key_col = pl.BlockSpec((resp, HD), lambda h: (0, h))
    contexts, key0, value0 = pl.pallas_call(
        response_kernel,
        grid=(heads,),
        in_specs=[
            head_col, head_col, head_col,
            pl.BlockSpec((shards, 2, rows, HD), lambda h: (0, 0, 0, h)),
            full, full, full,
        ],
        out_specs=[
            pl.BlockSpec((shards, STEPS, out_rows, HD), lambda h: (0, 0, 0, h)),
            key_col, key_col,
        ],
        out_shape=[
            jax.ShapeDtypeStruct((shards, STEPS, out_rows, local), jnp.bfloat16),
            jax.ShapeDtypeStruct((resp, local), jnp.bfloat16),
            jax.ShapeDtypeStruct((resp, local), jnp.bfloat16),
        ],
        scratch_shapes=[
            pltpu.VMEM((2 * resp, HD), jnp.float32),
            pltpu.VMEM((2 * resp, HD), jnp.float32),
            pltpu.VMEM((2 * resp, HD), jnp.float32),
            pltpu.VMEM((prompt, 2 * HD), jnp.bfloat16),
            pltpu.VMEM((resp, 2 * HD), jnp.bfloat16),
            pltpu.VMEM((2 * resp, 2 * HD), jnp.float32),
            pltpu.VMEM((2 * resp, HD), jnp.float32),
        ],
        compiler_params=params,
        cost_estimate=pl.CostEstimate(
            flops=4 * heads * HD * (2 * resp * prompt * 2 + STEPS * resp * resp),
            bytes_accessed=4 * prompt * local,
            transcendentals=heads * (2 * resp * prompt + STEPS * resp * resp),
        ),
    )(*proj, kv, cos_r, sin_r, commit_wide)

    got = lax.all_to_all(contexts, "seq", split_axis=0, concat_axis=0)
    my_rows = STEPS * out_rows
    ctx = jnp.transpose(got.reshape(shards, my_rows, local), (1, 0, 2)).reshape(my_rows, width)

    q_shards = max(1, math.gcd(shards, QBLOCK // rows))
    col_h = pl.BlockSpec((resp, HD), lambda h, i: (0, h))
    prompt_local = pl.pallas_call(
        prompt_kernel,
        grid=(heads, shards // q_shards),
        in_specs=[
            pl.BlockSpec((q_shards, rows, HD), lambda h, i: (i, 0, h)),
            pl.BlockSpec((shards, 2, rows, HD), lambda h, i: (0, 0, 0, h)),
            col_h, col_h,
        ],
        out_specs=pl.BlockSpec((q_shards, rows, HD), lambda h, i: (i, 0, h)),
        out_shape=jax.ShapeDtypeStruct((shards, rows, local), jnp.bfloat16),
        scratch_shapes=[pltpu.VMEM((prompt + resp, 2 * HD), jnp.bfloat16)],
        compiler_params=params,
        cost_estimate=pl.CostEstimate(
            flops=8 * heads * HD * prompt * (prompt + resp),
            bytes_accessed=8 * prompt * local,
            transcendentals=heads * prompt * (prompt + resp),
        ),
    )(q, kv, key0, value0)
    back = lax.all_to_all(prompt_local, "seq", split_axis=0, concat_axis=0)
    prompt_context = jnp.transpose(back, (1, 0, 2)).reshape(rows, width)

    def turn(x, by):
        return lax.ppermute(x, "groups", [(g, (g + by) % groups) for g in range(groups)])

    def project(x):
        return jnp.dot(x, all_w, preferred_element_type=jnp.float32).astype(jnp.bfloat16)

    mine, sib = [], []
    for by in range(groups):
        there = ctx if by == 0 else turn(ctx, by)
        beside = lax.ppermute(there, "seq", swap)
        out = project(jnp.concatenate([there, beside], axis=0))
        home = out if by == 0 else turn(out, groups - by)
        mine.append(home[:my_rows])
        sib.append(home[my_rows:])
    own_cols = jnp.stack(mine)
    other_cols = lax.ppermute(jnp.stack(sib), "seq", swap)
    pair = jnp.where(
        core == 0, jnp.stack([own_cols, other_cols], 2), jnp.stack([other_cols, own_cols], 2)
    )
    pair = lax.dynamic_slice_in_dim(
        jnp.concatenate([pair, pair], axis=0), lax.rem(groups - group, groups), groups, 0
    )
    attn = jnp.transpose(pair, (1, 0, 2, 3)).reshape(STEPS, out_rows, model).astype(jnp.float32)

    start = me * out_rows
    my_embed = lax.dynamic_slice_in_dim(response_embed, start, out_rows, 0)
    my_commit = lax.dynamic_slice_in_dim(commit_step, start, out_rows, 0)
    shown = my_commit[None, :, None] <= jnp.arange(STEPS)[:, None, None]
    inputs = jnp.where(shown, my_embed[None], mask_embed[None, None, :]).astype(jnp.float32)
    hidden = inputs + attn
    return (
        prompt_context,
        hidden.astype(jnp.bfloat16),
        rms_scale(hidden, residual_gain).astype(jnp.bfloat16),
    )


def solution(mesh):
    return jax.shard_map(
        per_device,
        mesh=mesh,
        in_specs=(
            P(("groups", "seq"), None),
            P(("groups", "seq"), None),
            P(("groups", "seq"), None),
            P("groups", None),
            P(),
            P("groups"),
            P("groups"),
            P(),
            P(),
            P(None, "seq"),
            P(None, "seq"),
            P(None, "seq"),
            P("seq", None),
        ),
        out_specs=(
            P(("groups", "seq"), None),
            P(None, ("groups", "seq"), None),
            P(None, ("groups", "seq"), None),
        ),
        check_vma=False,
    )
```

```python
import math

import jax
import jax.numpy as jnp
from jax import lax
from jax.experimental import pallas as pl
from jax.experimental.pallas import tpu as pltpu
from jax.sharding import PartitionSpec as P

HD = 128
STEPS = 4
ROPE_BASE = 500000.0
NORM_EPS = 1e-05
QBLOCK = 256
VMEM_LIMIT = 48 * 1024 * 1024
NT = (((1,), (1,)), ((), ()))


def rope_tables(positions):
    half = HD // 2
    exponent = jnp.arange(half, dtype=jnp.float32) * (2.0 / HD)
    inv_freq = ROPE_BASE ** (-exponent)
    angles = positions.astype(jnp.float32)[:, None] * inv_freq[None, :]
    cosine = jnp.cos(angles)
    sine = jnp.sin(angles)
    return jnp.concatenate([cosine, cosine], axis=-1), jnp.concatenate([-sine, sine], axis=-1)


def rms_scale(row_values, gain_row):
    return (
        row_values
        * lax.rsqrt(jnp.mean(row_values * row_values, axis=-1, keepdims=True) + NORM_EPS)
        * gain_row.astype(jnp.float32)
    )


def rope_in(x, cosine, sine):
    return x * cosine + pltpu.roll(x, HD // 2, 1) * sine


def query_factor():
    return math.log2(math.e) / math.sqrt(HD)


def kv_prep_kernel(key_ref, value_ref, cos_ref, sin_ref, kv_ref):
    for h in range(key_ref.shape[1] // HD):
        cols = slice(h * HD, (h + 1) * HD)
        kv_ref[0, 0, :, cols] = rope_in(
            key_ref[:, cols].astype(jnp.float32), cos_ref[...], sin_ref[...]
        ).astype(jnp.bfloat16)
    kv_ref[0, 1] = value_ref[...]


def q_prep_kernel(query_ref, cos_ref, sin_ref, q_ref):
    for h in range(query_ref.shape[1] // HD):
        cols = slice(h * HD, (h + 1) * HD)
        turned = rope_in(query_ref[:, cols].astype(jnp.float32), cos_ref[...], sin_ref[...])
        q_ref[0, :, cols] = (turned * query_factor()).astype(jnp.bfloat16)


def response_kernel(
    q_ref, k_ref, v_ref, kv_ref, cos_ref, sin_ref, commit_ref,
    out_ref, key0_ref, value0_ref,
    q_both, k_both, v_both, prompt_va, step_va, part_o, part_m,
):
    resp = cos_ref.shape[0]
    shards, _, rows, _ = kv_ref.shape
    prompt = shards * rows
    cosine, sine = cos_ref[...], sin_ref[...]

    def both(ref, dest, turn, factor):
        shown = ref[pl.ds(0, resp), :]
        hidden = jnp.broadcast_to(ref[pl.ds(resp, 1), :], (resp, HD))
        for slot, x in ((0, hidden), (1, shown)):
            if turn:
                x = rope_in(x, cosine, sine)
            dest[pl.ds(slot * resp, resp), :] = (x * factor).astype(jnp.bfloat16).astype(jnp.float32)

    both(q_ref, q_both, True, query_factor())
    both(k_ref, k_both, True, 1.0)
    both(v_ref, v_both, False, 1.0)
    prompt_va[:, :HD] = kv_ref[:, 1].reshape(prompt, HD)
    prompt_va[:, HD:] = jnp.ones((prompt, HD), jnp.bfloat16)
    step_va[:, HD:] = jnp.ones((resp, HD), jnp.bfloat16)
    block = math.gcd(QBLOCK, resp)

    def prompt_part(i, carry):
        at = pl.ds(pl.multiple_of(i * block, block), block)
        q = q_both[at, :].astype(jnp.bfloat16)
        k = kv_ref[:, 0].reshape(prompt, HD)
        s = lax.dot_general(q, k, NT, preferred_element_type=jnp.float32)
        m = jnp.max(s, axis=-1, keepdims=True)
        p = jnp.exp2(s - m).astype(jnp.bfloat16)
        part_o[at, :] = jnp.dot(p, prompt_va[...], preferred_element_type=jnp.float32)
        part_m[at, :] = jnp.broadcast_to(m, (block, HD))
        return carry

    lax.fori_loop(0, 2 * resp // block, prompt_part, 0)
    out_rows = out_ref.shape[2]
    for step in range(STEPS):
        shown = commit_ref[...] <= step
        k_s = jnp.where(shown, k_both[resp:, :], k_both[:resp, :]).astype(jnp.bfloat16)
        v_s = jnp.where(shown, v_both[resp:, :], v_both[:resp, :]).astype(jnp.bfloat16)
        step_va[:, :HD] = v_s
        if step == 0:
            key0_ref[...] = k_s
            value0_ref[...] = v_s
        for i in range(resp // block):
            lo, hi = i * block, (i + 1) * block
            here = commit_ref[lo:hi, :] <= step

            def pick(ref):
                return jnp.where(here, ref[resp + lo : resp + hi, :HD], ref[lo:hi, :HD])

            q = pick(q_both).astype(jnp.bfloat16)
            s = lax.dot_general(q, k_s, NT, preferred_element_type=jnp.float32)
            m_prompt = pick(part_m)
            m = jnp.maximum(jnp.max(s, axis=-1, keepdims=True), m_prompt)
            p = jnp.exp2(s - m[:, :1]).astype(jnp.bfloat16)
            o = jnp.dot(p, step_va[...], preferred_element_type=jnp.float32)
            shrink = jnp.exp2(m_prompt - m)
            top = o[:, :HD] + shrink * pick(part_o)
            total = o[:, HD:] + shrink * jnp.where(
                here, part_o[resp + lo : resp + hi, HD:], part_o[lo:hi, HD:]
            )
            out_ref[lo // out_rows : hi // out_rows, step] = (
                (top / total).astype(jnp.bfloat16).reshape(block // out_rows, out_rows, HD)
            )


def prompt_kernel(q_ref, kv_ref, key0_ref, value0_ref, out_ref, va):
    shards, _, rows, _ = kv_ref.shape
    prompt = shards * rows

    @pl.when(pl.program_id(1) == 0)
    def _():
        va[:prompt, :HD] = kv_ref[:, 1].reshape(prompt, HD)
        va[prompt:, :HD] = value0_ref[...]
        va[:, HD:] = jnp.ones((va.shape[0], HD), jnp.bfloat16)

    q = q_ref[...].reshape(-1, HD)
    s1 = lax.dot_general(
        q, kv_ref[:, 0].reshape(prompt, HD), NT, preferred_element_type=jnp.float32
    )
    s2 = lax.dot_general(q, key0_ref[...], NT, preferred_element_type=jnp.float32)
    m = jnp.maximum(jnp.max(s1, axis=-1, keepdims=True), jnp.max(s2, axis=-1, keepdims=True))
    p1 = jnp.exp2(s1 - m).astype(jnp.bfloat16)
    p2 = jnp.exp2(s2 - m).astype(jnp.bfloat16)
    o = jnp.dot(p1, va[:prompt, :], preferred_element_type=jnp.float32)
    o += jnp.dot(p2, va[prompt:, :], preferred_element_type=jnp.float32)
    out_ref[...] = (o[:, :HD] / o[:, HD:]).astype(jnp.bfloat16).reshape(out_ref.shape)


def finish_kernel(
    at_ref, own_ref, other_ref, embed_ref, mask_ref, commit_ref, gain_ref,
    residual_ref, normed_ref, hidden,
):
    groups, _, share = own_ref.shape
    group, core = at_ref[0], at_ref[1]
    for by in range(groups):
        first = lax.rem(group + by, groups) * 2
        for ref, c in ((own_ref, core), (other_ref, 1 - core)):
            at = pl.ds(pl.multiple_of((first + c) * share, share), share)
            hidden[:, at] = ref[by].astype(jnp.float32)
    shown = commit_ref[:, :1] <= pl.program_id(0)
    inputs = jnp.where(
        shown, embed_ref[...].astype(jnp.float32), mask_ref[...].astype(jnp.float32)
    )
    h = inputs + hidden[...]
    residual_ref[0] = h.astype(jnp.bfloat16)
    normed_ref[0] = rms_scale(h, gain_ref[...]).astype(jnp.bfloat16)


def per_device(
    prompt_query, prompt_key, prompt_value, response_embed, mask_embed, commit_step, block_index,
    attention_gain, residual_gain, query_weight, key_weight, value_weight, output_weight,
):
    rows, width = prompt_query.shape
    resp = response_embed.shape[0]
    model = response_embed.shape[1]
    shards = lax.axis_size("seq")
    groups = lax.axis_size("groups")
    me = lax.axis_index("seq")
    group = lax.axis_index("groups")
    cores = 2
    core = lax.rem(me, cores)
    local = query_weight.shape[1]
    heads = local // HD
    prompt = rows * shards
    params = pltpu.CompilerParams(vmem_limit_bytes=VMEM_LIMIT)
    swap = [(i, i ^ 1) for i in range(shards)]

    depth = output_weight.shape[0]
    share = model // (groups * cores)
    own_w = lax.dynamic_slice_in_dim(output_weight, (group * cores + core) * share, share, 1)
    give_w = lax.dynamic_slice_in_dim(output_weight, (group * cores + 1 - core) * share, share, 1)

    cos_p, sin_p = rope_tables(me * rows + jnp.arange(rows, dtype=jnp.int32))
    table = pl.BlockSpec((rows, HD), lambda s: (0, 0))
    column = pl.BlockSpec((rows, local), lambda s: (0, s))
    kv = pl.pallas_call(
        kv_prep_kernel,
        grid=(shards,),
        in_specs=[column, column, table, table],
        out_specs=pl.BlockSpec((1, 2, rows, local), lambda s: (s, 0, 0, 0)),
        out_shape=jax.ShapeDtypeStruct((shards, 2, rows, local), jnp.bfloat16),
        compiler_params=params,
    )(prompt_key, prompt_value, cos_p, sin_p)
    kv = lax.all_to_all(kv, "seq", split_axis=0, concat_axis=0)
    q_sent = pl.pallas_call(
        q_prep_kernel,
        grid=(shards,),
        in_specs=[column, table, table],
        out_specs=pl.BlockSpec((1, rows, local), lambda s: (s, 0, 0)),
        out_shape=jax.ShapeDtypeStruct((shards, rows, local), jnp.bfloat16),
        compiler_params=params,
    )(prompt_query, cos_p, sin_p)
    q = lax.all_to_all(q_sent, "seq", split_axis=0, concat_axis=0)

    got_w = lax.ppermute(give_w, "seq", swap)
    pair_w = jnp.where(core == 0, jnp.stack([own_w, got_w]), jnp.stack([got_w, own_w]))
    quad = 2 * cores
    lines = [[i for i in range(shards) if i % quad == c] for c in range(quad)]
    line_w = lax.all_gather(pair_w, "seq", axis=0, tiled=True, axis_index_groups=lines)
    line_w = line_w.reshape(width // 2, share)
    beside_w = lax.ppermute(line_w, "seq", [(i, i ^ cores) for i in range(shards)])

    both = jnp.concatenate(
        [response_embed, jnp.broadcast_to(mask_embed[None, :], (16, model))], axis=0
    )
    normed = rms_scale(both.astype(jnp.float32), attention_gain).astype(jnp.bfloat16)
    proj = [
        jnp.dot(normed, w, preferred_element_type=jnp.float32)
        for w in (query_weight, key_weight, value_weight)
    ]
    cos_r, sin_r = rope_tables(prompt + block_index[0] * resp + jnp.arange(resp, dtype=jnp.int32))
    commit_wide = jnp.broadcast_to(commit_step[:, None], (resp, HD))

    out_rows = resp // shards
    head_col = pl.BlockSpec((resp + 16, HD), lambda h: (0, h))
    full = pl.BlockSpec((resp, HD), lambda h: (0, 0))
    key_col = pl.BlockSpec((resp, HD), lambda h: (0, h))
    contexts, key0, value0 = pl.pallas_call(
        response_kernel,
        grid=(heads,),
        in_specs=[
            head_col, head_col, head_col,
            pl.BlockSpec((shards, 2, rows, HD), lambda h: (0, 0, 0, h)),
            full, full, full,
        ],
        out_specs=[
            pl.BlockSpec((shards, STEPS, out_rows, HD), lambda h: (0, 0, 0, h)),
            key_col, key_col,
        ],
        out_shape=[
            jax.ShapeDtypeStruct((shards, STEPS, out_rows, local), jnp.bfloat16),
            jax.ShapeDtypeStruct((resp, local), jnp.bfloat16),
            jax.ShapeDtypeStruct((resp, local), jnp.bfloat16),
        ],
        scratch_shapes=[
            pltpu.VMEM((2 * resp, HD), jnp.float32),
            pltpu.VMEM((2 * resp, HD), jnp.float32),
            pltpu.VMEM((2 * resp, HD), jnp.float32),
            pltpu.VMEM((prompt, 2 * HD), jnp.bfloat16),
            pltpu.VMEM((resp, 2 * HD), jnp.bfloat16),
            pltpu.VMEM((2 * resp, 2 * HD), jnp.float32),
            pltpu.VMEM((2 * resp, HD), jnp.float32),
        ],
        compiler_params=params,
        cost_estimate=pl.CostEstimate(
            flops=4 * heads * HD * (2 * resp * prompt * 2 + STEPS * resp * resp),
            bytes_accessed=4 * prompt * local,
            transcendentals=heads * (2 * resp * prompt + STEPS * resp * resp),
        ),
    )(*proj, kv, cos_r, sin_r, commit_wide)

    contexts, q = lax.optimization_barrier((contexts, q))
    got = lax.all_to_all(contexts, "seq", split_axis=0, concat_axis=0)
    my_rows = STEPS * out_rows
    pair_side = lax.rem(lax.div(me, cores), 2)
    got = got.reshape(shards // quad, 2, cores, my_rows, local)
    got = jnp.stack(
        [
            lax.dynamic_index_in_dim(got, pair_side, 1, keepdims=False),
            lax.dynamic_index_in_dim(got, 1 - pair_side, 1, keepdims=False),
        ]
    )
    ctx = jnp.transpose(got, (3, 0, 1, 2, 4)).reshape(my_rows, width)

    q_shards = max(1, math.gcd(shards, QBLOCK // rows))
    col_h = pl.BlockSpec((resp, HD), lambda h, i: (0, h))
    prompt_local = pl.pallas_call(
        prompt_kernel,
        grid=(heads, shards // q_shards),
        in_specs=[
            pl.BlockSpec((q_shards, rows, HD), lambda h, i: (i, 0, h)),
            pl.BlockSpec((shards, 2, rows, HD), lambda h, i: (0, 0, 0, h)),
            col_h, col_h,
        ],
        out_specs=pl.BlockSpec((q_shards, rows, HD), lambda h, i: (i, 0, h)),
        out_shape=jax.ShapeDtypeStruct((shards, rows, local), jnp.bfloat16),
        scratch_shapes=[pltpu.VMEM((prompt + resp, 2 * HD), jnp.bfloat16)],
        compiler_params=params,
        cost_estimate=pl.CostEstimate(
            flops=8 * heads * HD * prompt * (prompt + resp),
            bytes_accessed=8 * prompt * local,
            transcendentals=heads * prompt * (prompt + resp),
        ),
    )(q, kv, key0, value0)
    back = lax.all_to_all(prompt_local, "seq", split_axis=0, concat_axis=0)
    prompt_context = jnp.transpose(back, (1, 0, 2)).reshape(rows, width)

    def turn(x, by):
        return lax.ppermute(x, "groups", [(g, (g + by) % groups) for g in range(groups)])

    def project(x):
        near = jnp.dot(x[:, : width // 2], line_w, preferred_element_type=jnp.float32)
        far = jnp.dot(x[:, width // 2 :], beside_w, preferred_element_type=jnp.float32)
        return (near + far).astype(jnp.bfloat16)

    mine, sib = [], []
    for by in range(groups):
        there = ctx if by == 0 else turn(ctx, by)
        beside = lax.ppermute(there, "seq", swap)
        out = project(jnp.concatenate([there, beside], axis=0))
        home = out if by == 0 else turn(out, groups - by)
        mine.append(home[:my_rows])
        sib.append(home[my_rows:])
    own_cols = jnp.stack(mine)
    other_cols = lax.ppermute(jnp.stack(sib), "seq", swap)
    start = me * out_rows
    my_embed = lax.dynamic_slice_in_dim(response_embed, start, out_rows, 0)
    my_commit = lax.dynamic_slice_in_dim(commit_wide, start, out_rows, 0)
    part = pl.BlockSpec((groups, out_rows, share), lambda t, at: (0, t, 0))
    row = pl.BlockSpec((1, model), lambda t, at: (0, 0))
    result = pl.BlockSpec((1, out_rows, model), lambda t, at: (t, 0, 0))
    out_type = jax.ShapeDtypeStruct((STEPS, out_rows, model), jnp.bfloat16)
    residual, normed_rows = pl.pallas_call(
        finish_kernel,
        grid_spec=pltpu.PrefetchScalarGridSpec(
            num_scalar_prefetch=1,
            grid=(STEPS,),
            in_specs=[
                part, part,
                pl.BlockSpec((out_rows, model), lambda t, at: (0, 0)),
                row,
                pl.BlockSpec((out_rows, HD), lambda t, at: (0, 0)),
                row,
            ],
            out_specs=[result, result],
            scratch_shapes=[pltpu.VMEM((out_rows, model), jnp.float32)],
        ),
        out_shape=[out_type, out_type],
        compiler_params=params,
    )(
        jnp.stack([group, core]).astype(jnp.int32),
        own_cols, other_cols, my_embed, mask_embed[None, :], my_commit, residual_gain[None, :],
    )
    return prompt_context, residual, normed_rows


def solution(mesh):
    return jax.shard_map(
        per_device,
        mesh=mesh,
        in_specs=(
            P(("groups", "seq"), None),
            P(("groups", "seq"), None),
            P(("groups", "seq"), None),
            P("groups", None),
            P(),
            P("groups"),
            P("groups"),
            P(),
            P(),
            P(None, "seq"),
            P(None, "seq"),
            P(None, "seq"),
            P("seq", None),
        ),
        out_specs=(
            P(("groups", "seq"), None),
            P(None, ("groups", "seq"), None),
            P(None, ("groups", "seq"), None),
        ),
        check_vma=False,
    )
```

```python
import math

import jax
import jax.numpy as jnp
from jax import lax
from jax.experimental import pallas as pl
from jax.experimental.pallas import tpu as pltpu
from jax.sharding import PartitionSpec as P

HD = 128
STEPS = 4
ROPE_BASE = 500000.0
NORM_EPS = 1e-05
QBLOCK = 256
VMEM_LIMIT = 48 * 1024 * 1024
NT = (((1,), (1,)), ((), ()))


def rope_tables(positions):
    half = HD // 2
    exponent = jnp.arange(half, dtype=jnp.float32) * (2.0 / HD)
    inv_freq = ROPE_BASE ** (-exponent)
    angles = positions.astype(jnp.float32)[:, None] * inv_freq[None, :]
    cosine = jnp.cos(angles)
    sine = jnp.sin(angles)
    return jnp.concatenate([cosine, cosine], axis=-1), jnp.concatenate([-sine, sine], axis=-1)


def rms_scale(row_values, gain_row):
    return (
        row_values
        * lax.rsqrt(jnp.mean(row_values * row_values, axis=-1, keepdims=True) + NORM_EPS)
        * gain_row.astype(jnp.float32)
    )


def rope_in(x, cosine, sine):
    return x * cosine + pltpu.roll(x, HD // 2, 1) * sine


def query_factor():
    return math.log2(math.e) / math.sqrt(HD)


def kv_prep_kernel(key_ref, value_ref, cos_ref, sin_ref, kv_ref):
    for h in range(key_ref.shape[1] // HD):
        cols = slice(h * HD, (h + 1) * HD)
        kv_ref[0, 0, :, cols] = rope_in(
            key_ref[:, cols].astype(jnp.float32), cos_ref[...], sin_ref[...]
        ).astype(jnp.bfloat16)
    kv_ref[0, 1] = value_ref[...]


def q_prep_kernel(query_ref, cos_ref, sin_ref, q_ref):
    for h in range(query_ref.shape[1] // HD):
        cols = slice(h * HD, (h + 1) * HD)
        turned = rope_in(query_ref[:, cols].astype(jnp.float32), cos_ref[...], sin_ref[...])
        q_ref[0, :, cols] = (turned * query_factor()).astype(jnp.bfloat16)


def response_kernel(
    q_ref, k_ref, v_ref, kv_ref, cos_ref, sin_ref, commit_ref,
    out_ref, key0_ref, value0_ref,
    q_both, k_both, v_both, prompt_va, step_va, part_o, part_m,
):
    resp = cos_ref.shape[0]
    shards, _, rows, _ = kv_ref.shape
    prompt = shards * rows
    cosine, sine = cos_ref[...], sin_ref[...]

    def both(ref, dest, turn, factor):
        shown = ref[pl.ds(0, resp), :]
        hidden = jnp.broadcast_to(ref[pl.ds(resp, 1), :], (resp, HD))
        for slot, x in ((0, hidden), (1, shown)):
            if turn:
                x = rope_in(x, cosine, sine)
            dest[pl.ds(slot * resp, resp), :] = (x * factor).astype(jnp.bfloat16).astype(jnp.float32)

    both(q_ref, q_both, True, query_factor())
    both(k_ref, k_both, True, 1.0)
    both(v_ref, v_both, False, 1.0)
    prompt_va[:, :HD] = kv_ref[:, 1].reshape(prompt, HD)
    prompt_va[:, HD:] = jnp.ones((prompt, HD), jnp.bfloat16)
    step_va[:, HD:] = jnp.ones((resp, HD), jnp.bfloat16)
    block = math.gcd(QBLOCK, resp)

    def prompt_part(i, carry):
        at = pl.ds(pl.multiple_of(i * block, block), block)
        q = q_both[at, :].astype(jnp.bfloat16)
        k = kv_ref[:, 0].reshape(prompt, HD)
        s = lax.dot_general(q, k, NT, preferred_element_type=jnp.float32)
        m = jnp.max(s, axis=-1, keepdims=True)
        p = jnp.exp2(s - m).astype(jnp.bfloat16)
        part_o[at, :] = jnp.dot(p, prompt_va[...], preferred_element_type=jnp.float32)
        part_m[at, :] = jnp.broadcast_to(m, (block, HD))
        return carry

    lax.fori_loop(0, 2 * resp // block, prompt_part, 0)
    out_rows = out_ref.shape[2]
    for step in range(STEPS):
        shown = commit_ref[...] <= step
        k_s = jnp.where(shown, k_both[resp:, :], k_both[:resp, :]).astype(jnp.bfloat16)
        v_s = jnp.where(shown, v_both[resp:, :], v_both[:resp, :]).astype(jnp.bfloat16)
        step_va[:, :HD] = v_s
        if step == 0:
            key0_ref[...] = k_s
            value0_ref[...] = v_s
        for i in range(resp // block):
            lo, hi = i * block, (i + 1) * block
            here = commit_ref[lo:hi, :] <= step

            def pick(ref):
                return jnp.where(here, ref[resp + lo : resp + hi, :HD], ref[lo:hi, :HD])

            q = pick(q_both).astype(jnp.bfloat16)
            s = lax.dot_general(q, k_s, NT, preferred_element_type=jnp.float32)
            m_prompt = pick(part_m)
            m = jnp.maximum(jnp.max(s, axis=-1, keepdims=True), m_prompt)
            p = jnp.exp2(s - m[:, :1]).astype(jnp.bfloat16)
            o = jnp.dot(p, step_va[...], preferred_element_type=jnp.float32)
            shrink = jnp.exp2(m_prompt - m)
            top = o[:, :HD] + shrink * pick(part_o)
            total = o[:, HD:] + shrink * jnp.where(
                here, part_o[resp + lo : resp + hi, HD:], part_o[lo:hi, HD:]
            )
            out_ref[lo // out_rows : hi // out_rows, step] = (
                (top / total).astype(jnp.bfloat16).reshape(block // out_rows, out_rows, HD)
            )


def prompt_kernel(q_ref, kv_ref, key0_ref, value0_ref, out_ref, va):
    shards, _, rows, _ = kv_ref.shape
    prompt = shards * rows

    @pl.when(pl.program_id(1) == 0)
    def _():
        va[:prompt, :HD] = kv_ref[:, 1].reshape(prompt, HD)
        va[prompt:, :HD] = value0_ref[...]
        va[:, HD:] = jnp.ones((va.shape[0], HD), jnp.bfloat16)

    q = q_ref[...].reshape(-1, HD)
    s1 = lax.dot_general(
        q, kv_ref[:, 0].reshape(prompt, HD), NT, preferred_element_type=jnp.float32
    )
    s2 = lax.dot_general(q, key0_ref[...], NT, preferred_element_type=jnp.float32)
    m = jnp.maximum(jnp.max(s1, axis=-1, keepdims=True), jnp.max(s2, axis=-1, keepdims=True))
    p1 = jnp.exp2(s1 - m).astype(jnp.bfloat16)
    p2 = jnp.exp2(s2 - m).astype(jnp.bfloat16)
    o = jnp.dot(p1, va[:prompt, :], preferred_element_type=jnp.float32)
    o += jnp.dot(p2, va[prompt:, :], preferred_element_type=jnp.float32)
    out_ref[...] = (o[:, :HD] / o[:, HD:]).astype(jnp.bfloat16).reshape(out_ref.shape)


def finish_kernel(at_ref, *refs):
    groups = len(refs) - 7
    pieces = refs[:groups]
    embed_ref, mask_ref, commit_ref, gain_ref, residual_ref, normed_ref, hidden = refs[groups:]
    share = pieces[0].shape[1]
    for by, ref in enumerate(pieces):
        at = lax.rem(at_ref[0] + by, groups) * share
        hidden[:, pl.ds(pl.multiple_of(at, share), share)] = ref[...].astype(jnp.float32)
    shown = commit_ref[:, :1] <= pl.program_id(0)
    inputs = jnp.where(
        shown, embed_ref[...].astype(jnp.float32), mask_ref[...].astype(jnp.float32)
    )
    h = inputs + hidden[...]
    residual_ref[0] = h.astype(jnp.bfloat16)
    normed_ref[0] = rms_scale(h, gain_ref[...]).astype(jnp.bfloat16)


def per_device(
    prompt_query, prompt_key, prompt_value, response_embed, mask_embed, commit_step, block_index,
    attention_gain, residual_gain, query_weight, key_weight, value_weight, output_weight,
):
    rows, width = prompt_query.shape
    resp = response_embed.shape[0]
    model = response_embed.shape[1]
    shards = lax.axis_size("seq")
    groups = lax.axis_size("groups")
    me = lax.axis_index("seq")
    group = lax.axis_index("groups")
    local = query_weight.shape[1]
    heads = local // HD
    prompt = rows * shards
    params = pltpu.CompilerParams(vmem_limit_bytes=VMEM_LIMIT)

    share = model // groups
    own_w = lax.dynamic_slice_in_dim(output_weight, group * share, share, 1)
    all_w = lax.all_gather(own_w, "seq", axis=0, tiled=True)

    cos_p, sin_p = rope_tables(me * rows + jnp.arange(rows, dtype=jnp.int32))
    table = pl.BlockSpec((rows, HD), lambda s: (0, 0))
    column = pl.BlockSpec((rows, local), lambda s: (0, s))
    kv = pl.pallas_call(
        kv_prep_kernel,
        grid=(shards,),
        in_specs=[column, column, table, table],
        out_specs=pl.BlockSpec((1, 2, rows, local), lambda s: (s, 0, 0, 0)),
        out_shape=jax.ShapeDtypeStruct((shards, 2, rows, local), jnp.bfloat16),
        compiler_params=params,
    )(prompt_key, prompt_value, cos_p, sin_p)
    kv = lax.all_to_all(kv, "seq", split_axis=0, concat_axis=0)
    q_sent = pl.pallas_call(
        q_prep_kernel,
        grid=(shards,),
        in_specs=[column, table, table],
        out_specs=pl.BlockSpec((1, rows, local), lambda s: (s, 0, 0)),
        out_shape=jax.ShapeDtypeStruct((shards, rows, local), jnp.bfloat16),
        compiler_params=params,
    )(prompt_query, cos_p, sin_p)
    q = lax.all_to_all(q_sent, "seq", split_axis=0, concat_axis=0)

    both = jnp.concatenate(
        [response_embed, jnp.broadcast_to(mask_embed[None, :], (16, model))], axis=0
    )
    normed = rms_scale(both.astype(jnp.float32), attention_gain).astype(jnp.bfloat16)
    proj = [
        jnp.dot(normed, w, preferred_element_type=jnp.float32)
        for w in (query_weight, key_weight, value_weight)
    ]
    cos_r, sin_r = rope_tables(prompt + block_index[0] * resp + jnp.arange(resp, dtype=jnp.int32))
    commit_wide = jnp.broadcast_to(commit_step[:, None], (resp, HD))

    out_rows = resp // shards
    head_col = pl.BlockSpec((resp + 16, HD), lambda h: (0, h))
    full = pl.BlockSpec((resp, HD), lambda h: (0, 0))
    key_col = pl.BlockSpec((resp, HD), lambda h: (0, h))
    contexts, key0, value0 = pl.pallas_call(
        response_kernel,
        grid=(heads,),
        in_specs=[
            head_col, head_col, head_col,
            pl.BlockSpec((shards, 2, rows, HD), lambda h: (0, 0, 0, h)),
            full, full, full,
        ],
        out_specs=[
            pl.BlockSpec((shards, STEPS, out_rows, HD), lambda h: (0, 0, 0, h)),
            key_col, key_col,
        ],
        out_shape=[
            jax.ShapeDtypeStruct((shards, STEPS, out_rows, local), jnp.bfloat16),
            jax.ShapeDtypeStruct((resp, local), jnp.bfloat16),
            jax.ShapeDtypeStruct((resp, local), jnp.bfloat16),
        ],
        scratch_shapes=[
            pltpu.VMEM((2 * resp, HD), jnp.float32),
            pltpu.VMEM((2 * resp, HD), jnp.float32),
            pltpu.VMEM((2 * resp, HD), jnp.float32),
            pltpu.VMEM((prompt, 2 * HD), jnp.bfloat16),
            pltpu.VMEM((resp, 2 * HD), jnp.bfloat16),
            pltpu.VMEM((2 * resp, 2 * HD), jnp.float32),
            pltpu.VMEM((2 * resp, HD), jnp.float32),
        ],
        compiler_params=params,
        cost_estimate=pl.CostEstimate(
            flops=4 * heads * HD * (2 * resp * prompt * 2 + STEPS * resp * resp),
            bytes_accessed=4 * prompt * local,
            transcendentals=heads * (2 * resp * prompt + STEPS * resp * resp),
        ),
    )(*proj, kv, cos_r, sin_r, commit_wide)

    contexts, q = lax.optimization_barrier((contexts, q))
    got = lax.all_to_all(contexts, "seq", split_axis=0, concat_axis=0)
    my_rows = STEPS * out_rows
    got = got.reshape(shards, my_rows, local)

    q_shards = max(1, math.gcd(shards, QBLOCK // rows))
    col_h = pl.BlockSpec((resp, HD), lambda h, i: (0, h))
    prompt_local = pl.pallas_call(
        prompt_kernel,
        grid=(heads, shards // q_shards),
        in_specs=[
            pl.BlockSpec((q_shards, rows, HD), lambda h, i: (i, 0, h)),
            pl.BlockSpec((shards, 2, rows, HD), lambda h, i: (0, 0, 0, h)),
            col_h, col_h,
        ],
        out_specs=pl.BlockSpec((q_shards, rows, HD), lambda h, i: (i, 0, h)),
        out_shape=jax.ShapeDtypeStruct((shards, rows, local), jnp.bfloat16),
        scratch_shapes=[pltpu.VMEM((prompt + resp, 2 * HD), jnp.bfloat16)],
        compiler_params=params,
        cost_estimate=pl.CostEstimate(
            flops=8 * heads * HD * prompt * (prompt + resp),
            bytes_accessed=8 * prompt * local,
            transcendentals=heads * prompt * (prompt + resp),
        ),
    )(q, kv, key0, value0)
    got, prompt_local = lax.optimization_barrier((got, prompt_local))
    ctx = jnp.transpose(got, (1, 0, 2)).reshape(my_rows, width)
    back = lax.all_to_all(prompt_local, "seq", split_axis=0, concat_axis=0)
    prompt_context = jnp.transpose(back, (1, 0, 2)).reshape(rows, width)

    def turn(x, by):
        return lax.ppermute(x, "groups", [(g, (g + by) % groups) for g in range(groups)])

    pieces = []
    for by in range(groups):
        there = turn(ctx, by) if by else ctx
        out = jnp.dot(there, all_w, preferred_element_type=jnp.float32).astype(jnp.bfloat16)
        pieces.append(turn(out, groups - by) if by else out)

    start = me * out_rows
    my_embed = lax.dynamic_slice_in_dim(response_embed, start, out_rows, 0)
    my_commit = lax.dynamic_slice_in_dim(commit_wide, start, out_rows, 0)
    part = pl.BlockSpec((out_rows, share), lambda t, at: (t, 0))
    row = pl.BlockSpec((1, model), lambda t, at: (0, 0))
    result = pl.BlockSpec((1, out_rows, model), lambda t, at: (t, 0, 0))
    out_type = jax.ShapeDtypeStruct((STEPS, out_rows, model), jnp.bfloat16)
    residual, normed_rows = pl.pallas_call(
        finish_kernel,
        grid_spec=pltpu.PrefetchScalarGridSpec(
            num_scalar_prefetch=1,
            grid=(STEPS,),
            in_specs=[
                *[part] * groups,
                pl.BlockSpec((out_rows, model), lambda t, at: (0, 0)),
                row,
                pl.BlockSpec((out_rows, HD), lambda t, at: (0, 0)),
                row,
            ],
            out_specs=[result, result],
            scratch_shapes=[pltpu.VMEM((out_rows, model), jnp.float32)],
        ),
        out_shape=[out_type, out_type],
        compiler_params=params,
    )(
        group[None].astype(jnp.int32),
        *pieces, my_embed, mask_embed[None, :], my_commit, residual_gain[None, :],
    )
    return prompt_context, residual, normed_rows


def solution(mesh):
    return jax.shard_map(
        per_device,
        mesh=mesh,
        in_specs=(
            P(("groups", "seq"), None),
            P(("groups", "seq"), None),
            P(("groups", "seq"), None),
            P("groups", None),
            P(),
            P("groups"),
            P("groups"),
            P(),
            P(),
            P(None, "seq"),
            P(None, "seq"),
            P(None, "seq"),
            P("seq", None),
        ),
        out_specs=(
            P(("groups", "seq"), None),
            P(None, ("groups", "seq"), None),
            P(None, ("groups", "seq"), None),
        ),
        check_vma=False,
    )
```
